32 devices in a mesh: lon: 8 (over z, y), lat: 4 (over x, core).
Axes of the slice: x: 2, y: 2, z: 4, core: 2. Of those that a mesh axis runs over, the one named last changes fastest.
Arguments:
- queries: bfloat16 [4, 8, 384, 128], P('lat', 'lon'), may hold values from -4.6 to 4.6
- keys: bfloat16 [4, 8, 384, 128], P('lat', 'lon'), may hold values from -4.6 to 4.6
- values: bfloat16 [4, 8, 384, 128], P('lat', 'lon'), may hold values from -6 to 6
- cotangent: bfloat16 [4, 8, 384, 128], P('lat', 'lon'), may hold values from -384 to 384
- key_tiles: int32 [4, 8, 21], replicated, may hold values from 0 to 31, as said below
- tile_count: int32 [4, 8], replicated, may hold values from 2 to 21, as said below
Outputs:
- grad_queries: bfloat16 [4, 8, 384, 128], P('lat', 'lon')
- grad_keys: bfloat16 [4, 8, 384, 128], P('lat', 'lon')
- grad_values: bfloat16 [4, 8, 384, 128], P('lat', 'lon')
The draws below stay inside these ranges and needn't reach their ends.
Inputs may be any that keep to these rules, and one draw needn't show every extreme that they name: `key_tiles`: entries are tile ids. The first tile_count entries of tile (a, b) are distinct, include (a, b) itself, and name tiles of bands a - 1 to a + 1 whose longitude lies within 3 tiles of b around the cycle; later entries are tile ids. `tile_count`: some tiles list all 21 entries.
All inputs are finite; a program needn't handle non-finite values.
Results may differ from the reference program's by a relative error of at most 0.0067.
Values may be sent and summed in bfloat16 or wider, within the bound.
A program may use at most 64 MiB of HBM per device.

```python
import jax
import jax.numpy as jnp
from jax import lax

HD = 128
TOK_DEV = 384
REACH = 3
SLOTS = 21
LAT_TILES = 4
LON_TILES = 8


def drawn_entries(key):
    array_shape = (LAT_TILES, LON_TILES, TOK_DEV, HD)
    return jnp.clip(jax.random.normal(key, array_shape, jnp.float32), -4.6, 4.6)


def draw_queries(key, part):
    entries = drawn_entries(jax.random.fold_in(key, 3))
    return entries.astype(jnp.bfloat16)


def draw_keys(key, part):
    entries = drawn_entries(jax.random.fold_in(key, 4))
    return entries.astype(jnp.bfloat16)


def tile_plan(key):
    base_key = jax.random.fold_in(key, 97)
    window_len = 2 * REACH + 1
    slot_count = 3 * window_len
    full_shape = (LAT_TILES, LON_TILES, slot_count)
    band_index = jnp.arange(LAT_TILES)[:, None, None]
    column_index = jnp.arange(LON_TILES)[None, :, None]
    candidate = jnp.arange(slot_count)[None, None, :]
    cand_band = band_index + candidate // window_len - 1
    cand_column = (column_index + candidate % window_len - REACH) % LON_TILES
    inside = jnp.broadcast_to((cand_band >= 0) & (cand_band < LAT_TILES), full_shape)
    cand_ids = jnp.broadcast_to(jnp.clip(cand_band, 0, LAT_TILES - 1) * LON_TILES + cand_column, full_shape)
    self_id = jnp.broadcast_to(band_index * LON_TILES + column_index, full_shape)
    priority = jax.random.randint(jax.random.fold_in(base_key, 1), full_shape, 0, 4096)
    rank_score = priority * slot_count + candidate
    rank_score = jnp.where(candidate == window_len + REACH, -1, rank_score)
    rank_score = jnp.where(inside, rank_score, 4096 * slot_count + candidate)
    ranking = jnp.argsort(rank_score, axis=-1)
    listed_ids = jnp.take_along_axis(jnp.where(inside, cand_ids, self_id), ranking, axis=-1)
    valid_count = jnp.sum(inside.astype(jnp.int32), axis=-1)
    band_row = jnp.arange(LAT_TILES)
    pole_gap = jnp.minimum(band_row, LAT_TILES - 1 - band_row)[:, None]
    ceiling = jnp.maximum(3, slot_count - 3 * (pole_gap - 1))
    least = jnp.maximum(2, ceiling // 2)
    raw_pick = jax.random.randint(jax.random.fold_in(base_key, 2), (LAT_TILES, LON_TILES), 0, 1 << 20)
    middle_count = least + raw_pick % (ceiling - least + 1)
    trim_pick = jax.random.randint(jax.random.fold_in(base_key, 3), (LAT_TILES, LON_TILES), 0, 3)
    first_column = jnp.arange(LON_TILES)[None, :] == 0
    polar_count = valid_count - jnp.where(first_column, 0, trim_pick)
    counted = jnp.where(pole_gap <= 1, polar_count, jnp.minimum(middle_count, valid_count))
    return (listed_ids.astype(jnp.int32), counted.astype(jnp.int32))


def draw_key_tiles(key, part):
    return tile_plan(key)[0]


def draw_tile_count(key, part):
    return tile_plan(key)[1]


def block_levels(rng, extent, pieces, low, largest):
    level = 1.0
    for dim, parts in pieces:
        steps = jax.random.uniform(jax.random.fold_in(jax.random.fold_in(rng, 6), dim), (parts,), jnp.float32, low / len(pieces), largest / len(pieces))
        level = level * jnp.repeat(jnp.exp(steps), extent[dim] // parts).reshape((-1,) + (1,) * (len(extent) - 1 - dim))
    return level


def centred(key, shape, width, bound, cuts=(), kind=jnp.bfloat16):
    result = jax.random.normal(key, shape, jnp.float32) * width
    if len(cuts) > 0:
        result = block_levels(key, shape, cuts, -0.22, 0.18) * result
    return jnp.clip(result, min=-bound, max=bound).astype(kind)


def setup_inputs(seed: int = 0) -> dict:
    streams_of = jax.random.split(jax.random.key(seed), 7)
    return {
        "queries": draw_queries(jax.random.fold_in(streams_of[6], 71), 0),
        "keys": draw_keys(jax.random.fold_in(streams_of[6], 71), 0),
        "values": centred(streams_of[2], (LAT_TILES, LON_TILES, TOK_DEV, HD), 1.0, 6.0, ((0, 4), (1, 8))),
        "cotangent": centred(streams_of[3], (LAT_TILES, LON_TILES, TOK_DEV, HD), 64.0, 384.0, ((0, 4), (1, 8))),
        "key_tiles": draw_key_tiles(jax.random.fold_in(streams_of[6], 71), 0),
        "tile_count": draw_tile_count(jax.random.fold_in(streams_of[6], 71), 0),
    }


NEG_BIG = -1.0e30


def reference(queries, keys, values, cotangent, key_tiles, tile_count):
    tiles = LAT_TILES * LON_TILES
    score_scale = HD ** -0.5
    flat_q = queries.reshape(tiles, TOK_DEV, HD)
    flat_k = keys.reshape(tiles, TOK_DEV, HD)
    flat_v = values.reshape(tiles, TOK_DEV, HD)
    flat_g = cotangent.reshape(tiles, TOK_DEV, HD)
    tile_table = key_tiles.reshape(tiles, SLOTS)
    tile_totals = tile_count.reshape(tiles)

    def per_tile(state_now, position):
        grad_k, grad_v = state_now
        chosen = tile_table[position]
        slot_live = jnp.arange(SLOTS, dtype=jnp.int32) < tile_totals[position]
        tile_queries = flat_q[position].astype(jnp.float32)
        tile_grads = flat_g[position].astype(jnp.float32)
        key_set = flat_k[chosen].astype(jnp.float32)
        value_set = flat_v[chosen].astype(jnp.float32)
        logits = jnp.einsum("qd,skd->qsk", tile_queries, key_set) * score_scale
        logits = jnp.where(slot_live[None, :, None], logits, NEG_BIG)
        row_max = jnp.max(logits, axis=(1, 2))
        row_sum = jnp.sum(jnp.exp(logits - row_max[:, None, None]), axis=(1, 2))
        log_norm = row_max + jnp.log(row_sum)
        probs = jnp.exp(logits - log_norm[:, None, None])
        grad_prob = jnp.einsum("qd,skd->qsk", tile_grads, value_set)
        delta_rows = jnp.sum(probs * grad_prob, axis=(1, 2))
        grad_logit = lax.optimization_barrier((probs * (grad_prob - delta_rows[:, None, None])).astype(jnp.bfloat16)).astype(jnp.float32)
        probs_low = lax.optimization_barrier(probs.astype(jnp.bfloat16)).astype(jnp.float32)
        grad_query = jnp.einsum("qsk,skd->qd", grad_logit, key_set) * score_scale
        key_part = jnp.einsum("qsk,qd->skd", grad_logit, tile_queries) * score_scale
        value_part = jnp.einsum("qsk,qd->skd", probs_low, tile_grads)
        key_part = jnp.where(slot_live[:, None, None], key_part, 0.0)
        value_part = jnp.where(slot_live[:, None, None], value_part, 0.0)
        grad_k = grad_k.at[chosen].add(key_part)
        grad_v = grad_v.at[chosen].add(value_part)
        return (grad_k, grad_v), grad_query

    start = jnp.zeros((tiles, TOK_DEV, HD), jnp.float32)
    (grad_k, grad_v), grad_q = lax.scan(per_tile, (start, start), jnp.arange(tiles, dtype=jnp.int32))
    shape_out = (LAT_TILES, LON_TILES, TOK_DEV, HD)
    return (grad_q.reshape(shape_out).astype(jnp.bfloat16), grad_k.reshape(shape_out).astype(jnp.bfloat16), grad_v.reshape(shape_out).astype(jnp.bfloat16))
```

```python
import functools

import jax
import jax.numpy as jnp
from jax import lax
from jax.experimental import pallas as pl
from jax.experimental.pallas import tpu as pltpu
from jax.sharding import PartitionSpec as P

MESH = pl.DeviceIdType.MESH
PAIR_STEPS = (0, 1, -1, 2)
BANDS = (0, -1, 1)
BAND_BACK = (0, 2, 1)
UNLISTED = -1e30
LOWEST = -1e20
LOG2E = 1.4426950408889634


def dot_rows(a, b):
    return lax.dot_general(a, b, (((1,), (1,)), ((), ())), preferred_element_type=jnp.float32)


def dot(a, b):
    return jnp.dot(a, b, preferred_element_type=jnp.float32)


def kernel(
    pairs, bands,
    q_ref, k_ref, v_ref, g_ref, list_ref, count_ref,
    dq_ref, dk_ref, dv_ref,
    qbuf, gbuf, kbuf, vbuf, kturn, pstore, gpstore, maxrow, bias, stats, stats_in,
    plow, dslow, dqacc, dkacc, dvacc, dqout, dqin, dkout, dvout, dkin, dvin,
    q_send, q_recv, g_send, g_recv, k_send, k_recv, v_send, v_recv, s_send, s_recv,
    dq_send, dq_recv, dk_send, dk_recv, dv_send, dv_recv,
):
    rows, width = q_ref.shape[2], q_ref.shape[3]
    scale = width ** -0.5
    scale2 = scale * LOG2E
    lon = lax.axis_index("lon")
    lat = lax.axis_index("lat")
    g = lon // 2
    p = lon % 2
    sign = 1 - 2 * p
    ring = 2 * pairs

    def along(step):
        return lax.rem(lon + 2 * sign * step + 2 * ring, ring)

    def column(e):
        return 2 * g + p + e * sign

    def has_band(place):
        below = jnp.where(place == 1, lat > 0, True)
        above = jnp.where(place == 2, lat < bands - 1, True)
        return jnp.logical_and(below, above)

    distances = sorted({e % pairs for e in range(-3, 4)} - {0})

    barrier = pltpu.get_barrier_semaphore()
    for e in distances:
        pl.semaphore_signal(barrier, inc=1, device_id={"lon": along(e), "lat": lat}, device_id_type=MESH)
    beside = [(e, place) for e in (0, 1) for place in range(3) if (e, place) != (0, 0)]
    for e, place in beside:
        @pl.when(has_band(place))
        def _(e=e, place=place):
            pl.semaphore_signal(
                barrier, inc=1,
                device_id={"lon": column(e), "lat": lat + BANDS[place]}, device_id_type=MESH,
            )

    qbuf[0] = q_ref[0, 0]
    gbuf[0] = g_ref[0, 0]
    kbuf[0] = k_ref[0, 0]
    vbuf[0] = v_ref[0, 0]

    slot = lax.broadcasted_iota(jnp.int32, (8, 1), 0)
    other = jnp.where(slot >= 3, 1, 0)
    place = slot - 3 * other
    band = lat + jnp.where(place == 0, 0, jnp.where(place == 1, -1, 1))
    key_ids = band * ring + 2 * g + p + other * sign
    entry = lax.broadcasted_iota(jnp.int32, (1, list_ref.shape[2]), 1)
    lane = lax.broadcasted_iota(jnp.int32, (1, ring), 1)
    counts = count_ref[pl.ds(lat, 1), :]
    for t, step in enumerate(PAIR_STEPS):
        where_q = along(step)
        count = jnp.sum(jnp.where(lane == where_q, counts, 0), axis=1, keepdims=True)
        mine = list_ref[lat, pl.ds(where_q, 1), :]
        hit = jnp.where((mine == key_ids) & (entry < count), 1.0, 0.0)
        found = jnp.max(hit, axis=1, keepdims=True)
        bias[t] = jnp.broadcast_to(jnp.where(found > 0.5, 0.0, UNLISTED), (8, rows))

    stats[0:4] = jnp.full((4, rows), LOWEST, jnp.float32)
    stats[4:16] = jnp.zeros((12, rows), jnp.float32)

    n_beside = 1 + 2 * (jnp.where(lat > 0, 1, 0) + jnp.where(lat < bands - 1, 1, 0))
    pl.semaphore_wait(barrier, len(distances) + n_beside)

    def remote(src, dst, send, recv, to_lon, to_lat):
        return pltpu.make_async_remote_copy(
            src_ref=src, dst_ref=dst, send_sem=send, recv_sem=recv,
            device_id={"lon": to_lon, "lat": to_lat}, device_id_type=MESH,
        )

    def key_copies(e, place):
        here, there = 3 * e + place, 3 * e + BAND_BACK[place]
        to = (column(e), lat + BANDS[place])
        return (
            remote(k_ref.at[0, 0], kbuf.at[there], k_send.at[here], k_recv.at[there], *to),
            remote(v_ref.at[0, 0], vbuf.at[there], v_send.at[here], v_recv.at[there], *to),
        )

    def query_copies(t):
        to = (along(-PAIR_STEPS[t]), lat)
        return (
            remote(q_ref.at[0, 0], qbuf.at[t], q_send.at[t], q_recv.at[t], *to),
            remote(g_ref.at[0, 0], gbuf.at[t], g_send.at[t], g_recv.at[t], *to),
        )

    for t in (1, 2, 3):
        for copy in query_copies(t):
            copy.start()
    for e, place in beside:
        @pl.when(has_band(place))
        def _(e=e, place=place):
            for copy in key_copies(e, place):
                copy.start()

    dqacc[...] = jnp.zeros_like(dqacc)
    dkacc[...] = jnp.zeros_like(dkacc)
    dvacc[...] = jnp.zeros_like(dvacc)

    def arrived(buf, index, recv):
        pltpu.make_async_copy(buf.at[index], buf.at[index], recv.at[index]).wait()

    chunks = [pl.ds(i, 128) for i in range(0, rows, 128)]

    def first_slot(t):
        return 3 if t == 3 else 0

    def stored(t, ks):
        return t * 6 + ks - first_slot(t)

    def first_pair(t, ks):
        index = stored(t, ks)
        logits = dot_rows(kbuf[ks], qbuf[t])
        pstore[index] = logits
        offset = bias[t, pl.ds(ks, 1), :]
        top = jnp.max(logits, axis=0, keepdims=True) * scale2 + offset
        old = stats[t:t + 1]
        new = jnp.maximum(old, top)
        shift = new - offset
        gpstore[index] = dot_rows(vbuf[ks], gbuf[t])
        total = jnp.zeros((1, rows), jnp.float32)
        weighted = jnp.zeros((1, rows), jnp.float32)
        for c in chunks:
            powers = jnp.exp2(pstore[index, c, :] * scale2 - shift)
            pstore[index, c, :] = powers
            total += jnp.sum(powers, axis=0, keepdims=True)
            weighted += jnp.sum(powers * gpstore[index, c, :], axis=0, keepdims=True)
        shrink = jnp.exp2(old - new)
        maxrow[pl.ds(index, 1), :] = new
        stats[t:t + 1] = new
        stats[4 + t:5 + t] = stats[4 + t:5 + t] * shrink + total
        stats[8 + t:9 + t] = stats[8 + t:9 + t] * shrink + weighted

    for t in range(4):
        if t > 0:
            arrived(qbuf, t, q_recv)
            arrived(gbuf, t, g_recv)

        def first_step(ks, carry, t=t):
            @pl.when(has_band(ks % 3))
            def _():
                if t == 0:
                    @pl.when(ks > 0)
                    def _():
                        arrived(kbuf, ks, k_recv)
                        arrived(vbuf, ks, v_recv)
                    kturn[ks] = kbuf[ks].astype(jnp.float32).T.astype(jnp.bfloat16)
                first_pair(t, ks)
            return carry

        lax.fori_loop(first_slot(t), 6, first_step, 0)

    def stat_copy(i, e):
        back = distances.index(-e % pairs)
        return remote(stats, stats_in.at[back], s_send.at[i], s_recv.at[back], along(e), lat)

    for i, e in enumerate(distances):
        stat_copy(i, e).start()
    for i, e in enumerate(distances):
        arrived(stats_in, i, s_recv)

    finals = []
    for t, step in enumerate(PAIR_STEPS):
        parts = [(stats[t:t + 1], stats[4 + t:5 + t], stats[8 + t:9 + t])]
        for i, e in enumerate(distances):
            for other_t, other_step in enumerate(PAIR_STEPS):
                if (other_step + e - step) % pairs == 0:
                    parts.append(tuple(
                        stats_in[i, r + other_t:r + other_t + 1, :] for r in (0, 4, 8)
                    ))
        top = functools.reduce(jnp.maximum, [m for m, _, _ in parts])
        total = sum(l * jnp.exp2(m - top) for m, l, _ in parts)
        weighted = sum(w * jnp.exp2(m - top) for m, _, w in parts)
        inverse = 1.0 / total
        finals.append((top, inverse, weighted * inverse))

    def second_pair(t, ks):
        index = stored(t, ks)
        top, inverse, delta = finals[t]
        factor = jnp.exp2(maxrow[pl.ds(index, 1), :] - top) * inverse
        for c in chunks:
            probs = pstore[index, c, :] * factor
            plow[c, :] = probs.astype(jnp.bfloat16)
            dslow[c, :] = (probs * (gpstore[index, c, :] - delta)).astype(jnp.bfloat16)
        dvacc[ks] += dot(plow[...], gbuf[t])
        dkacc[ks] += dot(dslow[...], qbuf[t])
        dqacc[t] += dot(kturn[ks], dslow[...])

    def query_grad_copy(t):
        return remote(
            dqout.at[t], dqin.at[t], dq_send.at[t], dq_recv.at[t], along(PAIR_STEPS[t]), lat
        )

    for t in (3, 1, 2):
        def second_step(ks, carry, t=t):
            @pl.when(has_band(ks % 3))
            def _():
                second_pair(t, ks)
            return carry

        lax.fori_loop(first_slot(t), 6, second_step, 0)
        dqout[t] = (dqacc[t] * scale).astype(jnp.bfloat16)
        query_grad_copy(t).start()

    def key_grad_copies(ks):
        e, place = ks // 3, ks % 3
        back = 3 * e + jnp.where(place == 0, 0, 3 - place)
        to = (column(e), lat + jnp.where(place == 0, 0, 2 * place - 3))
        return (
            remote(dkout.at[ks], dkin.at[back], dk_send.at[ks], dk_recv.at[back], *to),
            remote(dvout.at[ks], dvin.at[back], dv_send.at[ks], dv_recv.at[back], *to),
        )

    def last_step(i, carry):
        ks = 5 - i

        @pl.when(has_band(ks % 3))
        def _():
            second_pair(0, ks)

            @pl.when(ks > 0)
            def _():
                dkout[ks] = (dkacc[ks] * scale).astype(jnp.bfloat16)
                dvout[ks] = dvacc[ks].astype(jnp.bfloat16)
                for copy in key_grad_copies(ks):
                    copy.start()
        return carry

    lax.fori_loop(0, 6, last_step, 0)

    total = dqacc[0] * scale
    for t in (3, 1, 2):
        arrived(dqin, t, dq_recv)
        total += dqin[t].astype(jnp.float32)
    dq_ref[0, 0] = total.T.astype(jnp.bfloat16)

    dkacc[0] = dkacc[0] * scale
    for e, place in reversed(beside):
        @pl.when(has_band(place))
        def _(e=e, place=place):
            ks = 3 * e + place
            arrived(dkin, ks, dk_recv)
            arrived(dvin, ks, dv_recv)
            dkacc[0] += dkin[ks].astype(jnp.float32)
            dvacc[0] += dvin[ks].astype(jnp.float32)
    dk_ref[0, 0] = dkacc[0].astype(jnp.bfloat16)
    dv_ref[0, 0] = dvacc[0].astype(jnp.bfloat16)

    for t in (1, 2, 3):
        for copy in query_copies(t):
            copy.wait_send()
        query_grad_copy(t).wait_send()
    for i, e in enumerate(distances):
        stat_copy(i, e).wait_send()
    for e, place in beside:
        @pl.when(has_band(place))
        def _(e=e, place=place):
            for copy in key_copies(e, place) + key_grad_copies(3 * e + place):
                copy.wait_send()


def per_device(pairs, bands, queries, keys, values, cotangent, key_tiles, tile_count):
    rows, width = queries.shape[2], queries.shape[3]
    shape = jax.ShapeDtypeStruct(queries.shape, jnp.bfloat16)
    low, full = jnp.bfloat16, jnp.float32
    n_stats = len({e % pairs for e in range(-3, 4)} - {0})
    vmem = pl.BlockSpec(memory_space=pltpu.VMEM)
    dma = pltpu.SemaphoreType.DMA
    return pl.pallas_call(
        functools.partial(kernel, pairs, bands),
        out_shape=(shape, shape, shape),
        in_specs=[vmem] * 6,
        out_specs=(vmem, vmem, vmem),
        scratch_shapes=[
            pltpu.VMEM((4, rows, width), low),
            pltpu.VMEM((4, rows, width), low),
            pltpu.VMEM((6, rows, width), low),
            pltpu.VMEM((6, rows, width), low),
            pltpu.VMEM((6, width, rows), low),
            pltpu.VMEM((21, rows, rows), full),
            pltpu.VMEM((21, rows, rows), full),
            pltpu.VMEM((24, rows), full),
            pltpu.VMEM((4, 8, rows), full),
            pltpu.VMEM((16, rows), full),
            pltpu.VMEM((n_stats, 16, rows), full),
            pltpu.VMEM((rows, rows), low),
            pltpu.VMEM((rows, rows), low),
            pltpu.VMEM((4, width, rows), full),
            pltpu.VMEM((6, rows, width), full),
            pltpu.VMEM((6, rows, width), full),
            pltpu.VMEM((4, width, rows), low),
            pltpu.VMEM((4, width, rows), low),
            pltpu.VMEM((6, rows, width), low),
            pltpu.VMEM((6, rows, width), low),
            pltpu.VMEM((6, rows, width), low),
            pltpu.VMEM((6, rows, width), low),
            dma((4,)), dma((4,)), dma((4,)), dma((4,)),
            dma((6,)), dma((6,)), dma((6,)), dma((6,)),
            dma((n_stats,)), dma((n_stats,)),
            dma((4,)), dma((4,)),
            dma((6,)), dma((6,)), dma((6,)), dma((6,)),
        ],
        compiler_params=pltpu.CompilerParams(
            collective_id=0, has_side_effects=True, vmem_limit_bytes=48 * 1024 * 1024
        ),
    )(queries, keys, values, cotangent, key_tiles, tile_count)


def solution(mesh):
    tiles = P("lat", "lon", None, None)
    return jax.shard_map(
        functools.partial(per_device, mesh.shape["lon"] // 2, mesh.shape["lat"]),
        mesh=mesh,
        in_specs=(tiles, tiles, tiles, tiles, P(), P()),
        out_specs=(tiles, tiles, tiles),
        check_vma=False,
    )
```

```python
import functools

import jax
import jax.numpy as jnp
from jax import lax
from jax.experimental import pallas as pl
from jax.experimental.pallas import tpu as pltpu
from jax.sharding import PartitionSpec as P

MESH = pl.DeviceIdType.MESH
PAIR_STEPS = (0, 1, -1, 2)
BANDS = (0, -1, 1)
BAND_BACK = (0, 2, 1)
UNLISTED = -1e30
LOWEST = -1e20
LOG2E = 1.4426950408889634


def dot_rows(a, b):
    return lax.dot_general(a, b, (((1,), (1,)), ((), ())), preferred_element_type=jnp.float32)


def dot(a, b):
    return jnp.dot(a, b, preferred_element_type=jnp.float32)


def kernel(
    pairs, bands,
    q_ref, k_ref, v_ref, g_ref, list_hbm, count_hbm,
    out_ref,
    qbuf, gbuf, kbuf, vbuf, kturn, pstore, gpstore, maxrow, bias, stats, stats_in,
    plow, dslow, dqacc, dkacc, dvacc, dqout, dqin, dkout, dvout, dkin, dvin,
    q_send, q_recv, g_send, g_recv, k_send, k_recv, v_send, v_recv, s_send, s_recv,
    dq_send, dq_recv, dk_send, dk_recv, dv_send, dv_recv,
    list_ref, count_ref, fetch_sem,
):
    rows, width = q_ref.shape[2], q_ref.shape[3]
    scale = width ** -0.5
    scale2 = scale * LOG2E
    lon = lax.axis_index("lon")
    lat = lax.axis_index("lat")
    g = lon // 2
    p = lon % 2
    sign = 1 - 2 * p
    ring = 2 * pairs

    def along(step):
        return lax.rem(lon + 2 * sign * step + 2 * ring, ring)

    def column(e):
        return 2 * g + p + e * sign

    own = ((q_ref.at[0, 0], qbuf.at[0]), (k_ref.at[0, 0], kbuf.at[0]),
           (v_ref.at[0, 0], vbuf.at[0]), (g_ref.at[0, 0], gbuf.at[0]),
           (list_hbm, list_ref), (count_hbm, count_ref))
    fetches = [
        pltpu.make_async_copy(src, dst, fetch_sem.at[i]) for i, (src, dst) in enumerate(own)
    ]
    for fetch in fetches:
        fetch.start()

    def has_band(place):
        below = jnp.where(place == 1, lat > 0, True)
        above = jnp.where(place == 2, lat < bands - 1, True)
        return jnp.logical_and(below, above)

    distances = sorted({e % pairs for e in range(-3, 4)} - {0})

    barrier = pltpu.get_barrier_semaphore()
    for e in distances:
        pl.semaphore_signal(barrier, inc=1, device_id={"lon": along(e), "lat": lat}, device_id_type=MESH)
    beside = [(0, 1), (0, 2), (1, 0)]
    for e, place in beside:
        @pl.when(has_band(place))
        def _(e=e, place=place):
            pl.semaphore_signal(
                barrier, inc=1,
                device_id={"lon": column(e), "lat": lat + BANDS[place]}, device_id_type=MESH,
            )

    n_beside = 1 + jnp.where(lat > 0, 1, 0) + jnp.where(lat < bands - 1, 1, 0)
    pl.semaphore_wait(barrier, len(distances) + n_beside)

    def remote(src, dst, send, recv, to_lon, to_lat):
        return pltpu.make_async_remote_copy(
            src_ref=src, dst_ref=dst, send_sem=send, recv_sem=recv,
            device_id={"lon": to_lon, "lat": to_lat}, device_id_type=MESH,
        )

    def key_copies(e, place):
        here, there = 3 * e + place, 3 * e + BAND_BACK[place]
        passed = e == 1 and place > 0
        to = (lon if passed else column(e), lat + BANDS[place])
        k_src = kbuf.at[3] if passed else k_ref.at[0, 0]
        v_src = vbuf.at[3] if passed else v_ref.at[0, 0]
        return (
            remote(k_src, kbuf.at[there], k_send.at[here], k_recv.at[there], *to),
            remote(v_src, vbuf.at[there], v_send.at[here], v_recv.at[there], *to),
        )

    def query_copies(t):
        to = (along(-PAIR_STEPS[t]), lat)
        return (
            remote(q_ref.at[0, 0], qbuf.at[t], q_send.at[t], q_recv.at[t], *to),
            remote(g_ref.at[0, 0], gbuf.at[t], g_send.at[t], g_recv.at[t], *to),
        )

    for t in (1, 2, 3):
        for copy in query_copies(t):
            copy.start()
    for e, place in beside:
        @pl.when(has_band(place))
        def _(e=e, place=place):
            for copy in key_copies(e, place):
                copy.start()

    fetches[4].wait()
    fetches[5].wait()
    slot = lax.broadcasted_iota(jnp.int32, (8, 1), 0)
    other = jnp.where(slot >= 3, 1, 0)
    place = slot - 3 * other
    band = lat + jnp.where(place == 0, 0, jnp.where(place == 1, -1, 1))
    key_ids = band * ring + 2 * g + p + other * sign
    entry = lax.broadcasted_iota(jnp.int32, (1, list_ref.shape[2]), 1)
    lane = lax.broadcasted_iota(jnp.int32, (1, ring), 1)
    counts = count_ref[pl.ds(lat, 1), :]
    for t, step in enumerate(PAIR_STEPS):
        where_q = along(step)
        count = jnp.sum(jnp.where(lane == where_q, counts, 0), axis=1, keepdims=True)
        mine = list_ref[lat, pl.ds(where_q, 1), :]
        hit = jnp.where((mine == key_ids) & (entry < count), 1.0, 0.0)
        found = jnp.max(hit, axis=1, keepdims=True)
        bias[t] = jnp.broadcast_to(jnp.where(found > 0.5, 0.0, UNLISTED), (8, rows))

    stats[0:4] = jnp.full((4, rows), LOWEST, jnp.float32)
    stats[4:16] = jnp.zeros((12, rows), jnp.float32)

    dqacc[...] = jnp.zeros_like(dqacc)
    dkacc[...] = jnp.zeros_like(dkacc)
    dvacc[...] = jnp.zeros_like(dvacc)

    def arrived(buf, index, recv):
        pltpu.make_async_copy(buf.at[index], buf.at[index], recv.at[index]).wait()

    chunks = [pl.ds(i, 128) for i in range(0, rows, 128)]

    def first_slot(t):
        return 3 if t == 3 else 0

    def stored(t, ks):
        return t * 6 + ks - first_slot(t)

    def first_pair(t, ks):
        index = stored(t, ks)
        logits = dot_rows(kbuf[ks], qbuf[t])
        pstore[index] = logits
        offset = bias[t, pl.ds(ks, 1), :]
        top = jnp.max(logits, axis=0, keepdims=True) * scale2 + offset
        old = stats[t:t + 1]
        new = jnp.maximum(old, top)
        shift = new - offset
        gpstore[index] = dot_rows(vbuf[ks], gbuf[t])
        total = jnp.zeros((1, rows), jnp.float32)
        weighted = jnp.zeros((1, rows), jnp.float32)
        for c in chunks:
            powers = jnp.exp2(pstore[index, c, :] * scale2 - shift)
            pstore[index, c, :] = powers
            total += jnp.sum(powers, axis=0, keepdims=True)
            weighted += jnp.sum(powers * gpstore[index, c, :], axis=0, keepdims=True)
        shrink = jnp.exp2(old - new)
        maxrow[pl.ds(index, 1), :] = new
        stats[t:t + 1] = new
        stats[4 + t:5 + t] = stats[4 + t:5 + t] * shrink + total
        stats[8 + t:9 + t] = stats[8 + t:9 + t] * shrink + weighted

    for fetch in fetches[:4]:
        fetch.wait()

    def keys_arrive(ks):
        arrived(kbuf, ks, k_recv)
        arrived(vbuf, ks, v_recv)

    def turn(ks):
        kturn[ks] = kbuf[ks].astype(jnp.float32).T.astype(jnp.bfloat16)

    def first_pairs(t, start, stop, fresh=False):
        def step(ks, carry):
            @pl.when(has_band(ks % 3))
            def _():
                if fresh:
                    keys_arrive(ks)
                    turn(ks)
                first_pair(t, ks)
            return carry

        lax.fori_loop(start, stop, step, 0)

    turn(0)
    first_pair(0, 0)
    first_pairs(0, 1, 3, fresh=True)
    keys_arrive(3)
    for place in (1, 2):
        @pl.when(has_band(place))
        def _(place=place):
            for copy in key_copies(1, place):
                copy.start()
    turn(3)
    first_pair(0, 3)
    arrived(qbuf, 1, q_recv)
    arrived(gbuf, 1, g_recv)
    first_pairs(1, 0, 4)
    first_pairs(0, 4, 6, fresh=True)
    first_pairs(1, 4, 6)
    for t in (2, 3):
        arrived(qbuf, t, q_recv)
        arrived(gbuf, t, g_recv)
        first_pairs(t, first_slot(t), 6)

    def stat_copy(i, e):
        back = distances.index(-e % pairs)
        return remote(stats, stats_in.at[back], s_send.at[i], s_recv.at[back], along(e), lat)

    for i, e in enumerate(distances):
        stat_copy(i, e).start()
    for i, e in enumerate(distances):
        arrived(stats_in, i, s_recv)

    finals = []
    for t, step in enumerate(PAIR_STEPS):
        parts = [(stats[t:t + 1], stats[4 + t:5 + t], stats[8 + t:9 + t])]
        for i, e in enumerate(distances):
            for other_t, other_step in enumerate(PAIR_STEPS):
                if (other_step + e - step) % pairs == 0:
                    parts.append(tuple(
                        stats_in[i, r + other_t:r + other_t + 1, :] for r in (0, 4, 8)
                    ))
        top = functools.reduce(jnp.maximum, [m for m, _, _ in parts])
        total = sum(l * jnp.exp2(m - top) for m, l, _ in parts)
        weighted = sum(w * jnp.exp2(m - top) for m, _, w in parts)
        inverse = 1.0 / total
        finals.append((top, inverse, weighted * inverse))

    def second_pair(t, ks):
        index = stored(t, ks)
        top, inverse, delta = finals[t]
        factor = jnp.exp2(maxrow[pl.ds(index, 1), :] - top) * inverse
        for c in chunks:
            probs = pstore[index, c, :] * factor
            plow[c, :] = probs.astype(jnp.bfloat16)
            dslow[c, :] = (probs * (gpstore[index, c, :] - delta)).astype(jnp.bfloat16)
        dvacc[ks] += dot(plow[...], gbuf[t])
        dkacc[ks] += dot(dslow[...], qbuf[t])
        dqacc[t] += dot(kturn[ks], dslow[...])

    def query_grad_copy(t):
        return remote(
            dqout.at[t], dqin.at[t], dq_send.at[t], dq_recv.at[t], along(PAIR_STEPS[t]), lat
        )

    def send_query_grad(t):
        dqout[t] = (dqacc[t] * scale).astype(jnp.bfloat16)
        query_grad_copy(t).start()

    def key_grad_copies(ks):
        e, place = ks // 3, ks % 3
        back = 3 * e + BAND_BACK[place]
        to = (column(1) if ks == 3 else lon, lat + BANDS[place])
        return (
            remote(dkout.at[ks], dkin.at[back], dk_send.at[ks], dk_recv.at[back], *to),
            remote(dvout.at[ks], dvin.at[back], dv_send.at[ks], dv_recv.at[back], *to),
        )

    def send_key_grad(ks):
        dkout[ks] = (dkacc[ks] * scale).astype(jnp.bfloat16)
        dvout[ks] = dvacc[ks].astype(jnp.bfloat16)
        for copy in key_grad_copies(ks):
            copy.start()

    def second_pairs(t, start, stop):
        def step(ks, carry):
            @pl.when(has_band(ks % 3))
            def _():
                second_pair(t, ks)
            return carry

        lax.fori_loop(start, stop, step, 0)

    def add_key_grad(ks, into, factor):
        arrived(dkin, ks, dk_recv)
        arrived(dvin, ks, dv_recv)
        dkacc[into] += dkin[ks].astype(jnp.float32) * factor
        dvacc[into] += dvin[ks].astype(jnp.float32)

    second_pairs(3, 3, 6)
    send_query_grad(3)
    second_pairs(1, 3, 6)
    second_pairs(2, 3, 6)
    second_pairs(0, 3, 6)
    for place in (1, 2):
        @pl.when(has_band(place))
        def _(place=place):
            send_key_grad(3 + place)
    second_pairs(1, 0, 3)
    send_query_grad(1)
    for place in (1, 2):
        @pl.when(has_band(place))
        def _(place=place):
            add_key_grad(3 + place, 3, 1.0 / scale)
    send_key_grad(3)
    second_pairs(2, 0, 3)
    send_query_grad(2)
    second_pairs(0, 1, 3)
    for place in (1, 2):
        @pl.when(has_band(place))
        def _(place=place):
            send_key_grad(place)
    second_pair(0, 0)

    total = dqacc[0] * scale
    for t in (3, 1, 2):
        arrived(dqin, t, dq_recv)
        total += dqin[t].astype(jnp.float32)
    out_ref[0] = total.T.astype(jnp.bfloat16)

    add_key_grad(3, 0, 1.0 / scale)
    for place in (1, 2):
        @pl.when(has_band(place))
        def _(place=place):
            add_key_grad(place, 0, 1.0 / scale)
    out_ref[1] = (dkacc[0] * scale).astype(jnp.bfloat16)
    out_ref[2] = dvacc[0].astype(jnp.bfloat16)

    for t in (1, 2, 3):
        for copy in query_copies(t):
            copy.wait_send()
        query_grad_copy(t).wait_send()
    for i, e in enumerate(distances):
        stat_copy(i, e).wait_send()
    for e, place in beside + [(1, 1), (1, 2)]:
        @pl.when(has_band(place))
        def _(e=e, place=place):
            for copy in key_copies(e, place) + key_grad_copies(3 * e + place):
                copy.wait_send()


def per_device(pairs, bands, queries, keys, values, cotangent, key_tiles, tile_count):
    rows, width = queries.shape[2], queries.shape[3]
    low, full = jnp.bfloat16, jnp.float32
    n_stats = len({e % pairs for e in range(-3, 4)} - {0})
    vmem = pl.BlockSpec(memory_space=pltpu.VMEM)
    dma = pltpu.SemaphoreType.DMA
    grads = pl.pallas_call(
        functools.partial(kernel, pairs, bands),
        out_shape=jax.ShapeDtypeStruct((3, rows, width), low),
        in_specs=[pl.BlockSpec(memory_space=pl.ANY)] * 6,
        out_specs=vmem,
        scratch_shapes=[
            pltpu.VMEM((4, rows, width), low),
            pltpu.VMEM((4, rows, width), low),
            pltpu.VMEM((6, rows, width), low),
            pltpu.VMEM((6, rows, width), low),
            pltpu.VMEM((6, width, rows), low),
            pltpu.VMEM((21, rows, rows), full),
            pltpu.VMEM((21, rows, rows), full),
            pltpu.VMEM((24, rows), full),
            pltpu.VMEM((4, 8, rows), full),
            pltpu.VMEM((16, rows), full),
            pltpu.VMEM((n_stats, 16, rows), full),
            pltpu.VMEM((rows, rows), low),
            pltpu.VMEM((rows, rows), low),
            pltpu.VMEM((4, width, rows), full),
            pltpu.VMEM((6, rows, width), full),
            pltpu.VMEM((6, rows, width), full),
            pltpu.VMEM((4, width, rows), low),
            pltpu.VMEM((4, width, rows), low),
            pltpu.VMEM((6, rows, width), low),
            pltpu.VMEM((6, rows, width), low),
            pltpu.VMEM((6, rows, width), low),
            pltpu.VMEM((6, rows, width), low),
            dma((4,)), dma((4,)), dma((4,)), dma((4,)),
            dma((6,)), dma((6,)), dma((6,)), dma((6,)),
            dma((n_stats,)), dma((n_stats,)),
            dma((4,)), dma((4,)),
            dma((6,)), dma((6,)), dma((6,)), dma((6,)),
            pltpu.VMEM(key_tiles.shape, jnp.int32),
            pltpu.VMEM(tile_count.shape, jnp.int32),
            dma((6,)),
        ],
        compiler_params=pltpu.CompilerParams(
            collective_id=0, has_side_effects=True, vmem_limit_bytes=60 * 1024 * 1024
        ),
    )(queries, keys, values, cotangent, key_tiles, tile_count)
    return tuple(grads[i].reshape(queries.shape) for i in range(3))


def solution(mesh):
    tiles = P("lat", "lon", None, None)
    return jax.shard_map(
        functools.partial(per_device, mesh.shape["lon"] // 2, mesh.shape["lat"]),
        mesh=mesh,
        in_specs=(tiles, tiles, tiles, tiles, P(), P()),
        out_specs=(tiles, tiles, tiles),
        check_vma=False,
    )
```

```python
import functools

import jax
import jax.numpy as jnp
from jax import lax
from jax.experimental import pallas as pl
from jax.experimental.pallas import tpu as pltpu
from jax.sharding import PartitionSpec as P

MESH = pl.DeviceIdType.MESH
PAIR_STEPS = (0, 1, -1, 2)
BANDS = (0, -1, 1)
BAND_BACK = (0, 2, 1)
UNLISTED = -1e30
LOWEST = -1e20
LOG2E = 1.4426950408889634


def dot_rows(a, b):
    return lax.dot_general(a, b, (((1,), (1,)), ((), ())), preferred_element_type=jnp.float32)


def dot(a, b):
    return jnp.dot(a, b, preferred_element_type=jnp.float32)


def kernel(
    pairs, bands,
    q_ref, k_ref, v_ref, g_ref, list_hbm, count_hbm,
    out_ref,
    qbuf, gbuf, kbuf, vbuf, kturn, pstore, gpstore, maxrow, bias, stats, stats_in,
    plow, dslow, dqacc, dkacc, dvacc, dqout, dqin, dkout, dvout, dkin, dvin,
    q_send, q_recv, g_send, g_recv, k_send, k_recv, v_send, v_recv, s_send, s_recv,
    dq_send, dq_recv, dk_send, dk_recv, dv_send, dv_recv,
    list_ref, count_ref, fetch_sem,
):
    rows, width = q_ref.shape[2], q_ref.shape[3]
    scale = width ** -0.5
    scale2 = scale * LOG2E
    lon = lax.axis_index("lon")
    lat = lax.axis_index("lat")
    g = lon // 2
    p = lon % 2
    sign = 1 - 2 * p
    ring = 2 * pairs

    def along(step):
        return lax.rem(lon + 2 * sign * step + 2 * ring, ring)

    def column(e):
        return 2 * g + p + e * sign

    own = ((q_ref.at[0, 0], qbuf.at[0]), (k_ref.at[0, 0], kbuf.at[0]),
           (v_ref.at[0, 0], vbuf.at[0]), (g_ref.at[0, 0], gbuf.at[0]),
           (list_hbm, list_ref), (count_hbm, count_ref))
    fetches = [
        pltpu.make_async_copy(src, dst, fetch_sem.at[i]) for i, (src, dst) in enumerate(own)
    ]
    for fetch in fetches:
        fetch.start()

    def has_band(place):
        below = jnp.where(place == 1, lat > 0, True)
        above = jnp.where(place == 2, lat < bands - 1, True)
        return jnp.logical_and(below, above)

    distances = sorted({e % pairs for e in range(-3, 4)} - {0})

    barrier = pltpu.get_barrier_semaphore()
    for e in distances:
        pl.semaphore_signal(barrier, inc=1, device_id={"lon": along(e), "lat": lat}, device_id_type=MESH)
    beside = [(0, 1), (0, 2), (1, 0)]
    for e, place in beside:
        @pl.when(has_band(place))
        def _(e=e, place=place):
            pl.semaphore_signal(
                barrier, inc=1,
                device_id={"lon": column(e), "lat": lat + BANDS[place]}, device_id_type=MESH,
            )

    n_beside = 1 + jnp.where(lat > 0, 1, 0) + jnp.where(lat < bands - 1, 1, 0)
    pl.semaphore_wait(barrier, len(distances) + n_beside)

    def remote(src, dst, send, recv, to_lon, to_lat):
        return pltpu.make_async_remote_copy(
            src_ref=src, dst_ref=dst, send_sem=send, recv_sem=recv,
            device_id={"lon": to_lon, "lat": to_lat}, device_id_type=MESH,
        )

    def key_copies(e, place):
        here, there = 3 * e + place, 3 * e + BAND_BACK[place]
        passed = e == 1 and place > 0
        to = (lon if passed else column(e), lat + BANDS[place])
        k_src = kbuf.at[3] if passed else k_ref.at[0, 0]
        v_src = vbuf.at[3] if passed else v_ref.at[0, 0]
        return (
            remote(k_src, kbuf.at[there], k_send.at[here], k_recv.at[there], *to),
            remote(v_src, vbuf.at[there], v_send.at[here], v_recv.at[there], *to),
        )

    def query_copies(t):
        to = (along(-PAIR_STEPS[t]), lat)
        return (
            remote(q_ref.at[0, 0], qbuf.at[t], q_send.at[t], q_recv.at[t], *to),
            remote(g_ref.at[0, 0], gbuf.at[t], g_send.at[t], g_recv.at[t], *to),
        )

    for t in (1, 2, 3):
        for copy in query_copies(t):
            copy.start()
    for e, place in beside:
        @pl.when(has_band(place))
        def _(e=e, place=place):
            for copy in key_copies(e, place):
                copy.start()

    fetches[4].wait()
    fetches[5].wait()
    slot = lax.broadcasted_iota(jnp.int32, (8, 1), 0)
    other = jnp.where(slot >= 3, 1, 0)
    place = slot - 3 * other
    band = lat + jnp.where(place == 0, 0, jnp.where(place == 1, -1, 1))
    key_ids = band * ring + 2 * g + p + other * sign
    entry = lax.broadcasted_iota(jnp.int32, (1, list_ref.shape[2]), 1)
    lane = lax.broadcasted_iota(jnp.int32, (1, ring), 1)
    counts = count_ref[pl.ds(lat, 1), :]
    for t, step in enumerate(PAIR_STEPS):
        where_q = along(step)
        count = jnp.sum(jnp.where(lane == where_q, counts, 0), axis=1, keepdims=True)
        mine = list_ref[lat, pl.ds(where_q, 1), :]
        hit = jnp.where((mine == key_ids) & (entry < count), 1.0, 0.0)
        found = jnp.max(hit, axis=1, keepdims=True)
        bias[t] = jnp.broadcast_to(jnp.where(found > 0.5, 0.0, UNLISTED), (8, rows))

    stats[0:4] = jnp.full((4, rows), LOWEST, jnp.float32)
    stats[4:16] = jnp.zeros((12, rows), jnp.float32)

    dqacc[...] = jnp.zeros_like(dqacc)

    def arrived(buf, index, recv):
        pltpu.make_async_copy(buf.at[index], buf.at[index], recv.at[index]).wait()

    chunks = [pl.ds(i, 32) for i in range(0, rows, 32)]

    def first_slot(t):
        return 3 if t == 3 else 0

    def stored(t, ks):
        return t * 6 + ks - first_slot(t)

    def first_pair(t, ks):
        index = stored(t, ks)
        logits = dot_rows(kbuf[ks], qbuf[t])
        pstore[index] = logits
        offset = bias[t, pl.ds(ks, 1), :]
        top = jnp.max(logits, axis=0, keepdims=True) * scale2 + offset
        old = stats[t:t + 1]
        new = jnp.maximum(old, top)
        shift = new - offset
        gpstore[index] = dot_rows(vbuf[ks], gbuf[t])
        total = jnp.zeros((8, rows), jnp.float32)
        weighted = jnp.zeros((8, rows), jnp.float32)
        for c in chunks:
            powers = jnp.exp2(pstore[index, c, :] * scale2 - shift)
            pstore[index, c, :] = powers
            total += jnp.sum(powers.reshape(-1, 8, rows), axis=0)
            terms = powers * gpstore[index, c, :]
            weighted += jnp.sum(terms.reshape(-1, 8, rows), axis=0)
        total = jnp.sum(total, axis=0, keepdims=True)
        weighted = jnp.sum(weighted, axis=0, keepdims=True)
        shrink = jnp.exp2(old - new)
        maxrow[pl.ds(index, 1), :] = new
        stats[t:t + 1] = new
        stats[4 + t:5 + t] = stats[4 + t:5 + t] * shrink + total
        stats[8 + t:9 + t] = stats[8 + t:9 + t] * shrink + weighted

    for fetch in fetches[:4]:
        fetch.wait()

    def keys_arrive(ks):
        arrived(kbuf, ks, k_recv)
        arrived(vbuf, ks, v_recv)

    def turn(ks):
        kturn[ks] = kbuf[ks].astype(jnp.float32).T.astype(jnp.bfloat16)

    def first_pairs(ts, start, stop, fresh=False):
        def step(ks, carry):
            @pl.when(has_band(ks % 3))
            def _():
                if fresh:
                    keys_arrive(ks)
                    turn(ks)
                for t in ts:
                    first_pair(t, ks)
            return carry

        lax.fori_loop(start, stop, step, 0)

    turn(0)
    first_pair(0, 0)
    first_pairs((0,), 1, 3, fresh=True)
    keys_arrive(3)
    for place in (1, 2):
        @pl.when(has_band(place))
        def _(place=place):
            for copy in key_copies(1, place):
                copy.start()
    turn(3)
    first_pair(0, 3)
    first_pairs((0,), 4, 6, fresh=True)
    for ts in ((1, 2), (3,)):
        for t in ts:
            arrived(qbuf, t, q_recv)
            arrived(gbuf, t, g_recv)
        first_pairs(ts, first_slot(ts[0]), 6)

    def stat_copy(i, e):
        back = distances.index(-e % pairs)
        return remote(stats, stats_in.at[back], s_send.at[i], s_recv.at[back], along(e), lat)

    for i, e in enumerate(distances):
        stat_copy(i, e).start()
    for i, e in enumerate(distances):
        arrived(stats_in, i, s_recv)

    finals = []
    for t, step in enumerate(PAIR_STEPS):
        parts = [(stats[t:t + 1], stats[4 + t:5 + t], stats[8 + t:9 + t])]
        for i, e in enumerate(distances):
            for other_t, other_step in enumerate(PAIR_STEPS):
                if (other_step + e - step) % pairs == 0:
                    parts.append(tuple(
                        stats_in[i, r + other_t:r + other_t + 1, :] for r in (0, 4, 8)
                    ))
        top = functools.reduce(jnp.maximum, [m for m, _, _ in parts])
        total = sum(l * jnp.exp2(m - top) for m, l, _ in parts)
        weighted = sum(w * jnp.exp2(m - top) for m, _, w in parts)
        inverse = 1.0 / total
        finals.append((top, inverse, weighted * inverse))

    def low_terms(t, ks):
        index = stored(t, ks)
        top, inverse, delta = finals[t]
        factor = jnp.exp2(maxrow[pl.ds(index, 1), :] - top) * inverse
        columns = slice(t * rows, (t + 1) * rows)
        for c in chunks:
            probs = pstore[index, c, :] * factor
            plow[c, columns] = probs.astype(jnp.bfloat16)
            dslow[c, columns] = (probs * (gpstore[index, c, :] - delta)).astype(jnp.bfloat16)

    def products(first, count, ks):
        columns = slice(first * rows, (first + count) * rows)
        dqacc[:, columns] += dot(kturn[ks], dslow[:, columns])
        value_part = dot(plow[:, columns], gbuf[first:first + count].reshape(-1, width))
        key_part = dot(dslow[:, columns], qbuf[first:first + count].reshape(-1, width))
        return key_part, value_part

    def query_grad_copy(t):
        return remote(
            dqout.at[t], dqin.at[t], dq_send.at[t], dq_recv.at[t], along(PAIR_STEPS[t]), lat
        )

    def send_query_grad(t):
        dqout[t] = (dqacc[:, t * rows:(t + 1) * rows] * scale).astype(jnp.bfloat16)
        query_grad_copy(t).start()

    def key_grad_copies(ks):
        e, place = ks // 3, ks % 3
        back = 3 * e + jnp.where(place == 0, 0, 3 - place)
        to = (jnp.where(ks == 3, column(1), lon), lat + jnp.where(place == 0, 0, 2 * place - 3))
        return (
            remote(dkout.at[ks], dkin.at[back], dk_send.at[ks], dk_recv.at[back], *to),
            remote(dvout.at[ks], dvin.at[back], dv_send.at[ks], dv_recv.at[back], *to),
        )

    def send_key_grad(ks):
        dkout[ks] = (dkacc[ks] * scale).astype(jnp.bfloat16)
        dvout[ks] = dvacc[ks].astype(jnp.bfloat16)
        for copy in key_grad_copies(ks):
            copy.start()

    def add_key_grad(ks, into, factor):
        arrived(dkin, ks, dk_recv)
        arrived(dvin, ks, dv_recv)
        dkacc[into] += dkin[ks].astype(jnp.float32) * factor
        dvacc[into] += dvin[ks].astype(jnp.float32)

    def other_parity(i, carry):
        place = (i + 1) % 3
        ks = 3 + place

        @pl.when(has_band(place))
        def _():
            for t in (3, 2, 1, 0):
                low_terms(t, ks)
            key_late, value_late = products(2, 2, ks)
            key_early, value_early = products(0, 2, ks)
            dkacc[ks] = key_late + key_early
            dvacc[ks] = value_late + value_early

            @pl.when(place > 0)
            def _():
                send_key_grad(ks)
        return carry

    lax.fori_loop(0, 3, other_parity, 0)
    send_query_grad(3)

    def neighbours(ks):
        for t in (1, 2):
            low_terms(t, ks)
        dkacc[ks], dvacc[ks] = products(1, 2, ks)

    neighbours(0)
    for place in (1, 2):
        @pl.when(has_band(place))
        def _(place=place):
            add_key_grad(3 + place, 3, 1.0 / scale)
    send_key_grad(3)

    def same_parity(ks, carry):
        @pl.when(has_band(ks))
        def _():
            neighbours(ks)
        return carry

    lax.fori_loop(1, 3, same_parity, 0)
    send_query_grad(1)
    send_query_grad(2)

    def own_queries(i, carry):
        ks = (i + 1) % 3

        @pl.when(has_band(ks))
        def _():
            low_terms(0, ks)
            key_part, value_part = products(0, 1, ks)
            dkacc[ks] += key_part
            dvacc[ks] += value_part

            @pl.when(ks > 0)
            def _():
                send_key_grad(ks)
        return carry

    lax.fori_loop(0, 3, own_queries, 0)

    total = dqacc[:, :rows] * scale
    for t in (3, 1, 2):
        arrived(dqin, t, dq_recv)
        total += dqin[t].astype(jnp.float32)
    out_ref[0] = total.T.astype(jnp.bfloat16)

    add_key_grad(3, 0, 1.0 / scale)
    for place in (1, 2):
        @pl.when(has_band(place))
        def _(place=place):
            add_key_grad(place, 0, 1.0 / scale)
    out_ref[1] = (dkacc[0] * scale).astype(jnp.bfloat16)
    out_ref[2] = dvacc[0].astype(jnp.bfloat16)

    for t in (1, 2, 3):
        for copy in query_copies(t):
            copy.wait_send()
        query_grad_copy(t).wait_send()
    for i, e in enumerate(distances):
        stat_copy(i, e).wait_send()
    for e, place in beside + [(1, 1), (1, 2)]:
        @pl.when(has_band(place))
        def _(e=e, place=place):
            for copy in key_copies(e, place) + key_grad_copies(3 * e + place):
                copy.wait_send()


def per_device(pairs, bands, queries, keys, values, cotangent, key_tiles, tile_count):
    rows, width = queries.shape[2], queries.shape[3]
    low, full = jnp.bfloat16, jnp.float32
    n_stats = len({e % pairs for e in range(-3, 4)} - {0})
    vmem = pl.BlockSpec(memory_space=pltpu.VMEM)
    dma = pltpu.SemaphoreType.DMA
    grads = pl.pallas_call(
        functools.partial(kernel, pairs, bands),
        out_shape=jax.ShapeDtypeStruct((3, rows, width), low),
        in_specs=[pl.BlockSpec(memory_space=pl.ANY)] * 6,
        out_specs=vmem,
        scratch_shapes=[
            pltpu.VMEM((4, rows, width), low),
            pltpu.VMEM((4, rows, width), low),
            pltpu.VMEM((6, rows, width), low),
            pltpu.VMEM((6, rows, width), low),
            pltpu.VMEM((6, width, rows), low),
            pltpu.VMEM((21, rows, rows), full),
            pltpu.VMEM((21, rows, rows), full),
            pltpu.VMEM((24, rows), full),
            pltpu.VMEM((4, 8, rows), full),
            pltpu.VMEM((16, rows), full),
            pltpu.VMEM((n_stats, 16, rows), full),
            pltpu.VMEM((rows, 4 * rows), low),
            pltpu.VMEM((rows, 4 * rows), low),
            pltpu.VMEM((width, 4 * rows), full),
            pltpu.VMEM((6, rows, width), full),
            pltpu.VMEM((6, rows, width), full),
            pltpu.VMEM((4, width, rows), low),
            pltpu.VMEM((4, width, rows), low),
            pltpu.VMEM((6, rows, width), low),
            pltpu.VMEM((6, rows, width), low),
            pltpu.VMEM((6, rows, width), low),
            pltpu.VMEM((6, rows, width), low),
            dma((4,)), dma((4,)), dma((4,)), dma((4,)),
            dma((6,)), dma((6,)), dma((6,)), dma((6,)),
            dma((n_stats,)), dma((n_stats,)),
            dma((4,)), dma((4,)),
            dma((6,)), dma((6,)), dma((6,)), dma((6,)),
            pltpu.VMEM(key_tiles.shape, jnp.int32),
            pltpu.VMEM(tile_count.shape, jnp.int32),
            dma((6,)),
        ],
        compiler_params=pltpu.CompilerParams(
            collective_id=0, has_side_effects=True, vmem_limit_bytes=60 * 1024 * 1024
        ),
    )(queries, keys, values, cotangent, key_tiles, tile_count)
    return tuple(grads[i].reshape(queries.shape) for i in range(3))


def solution(mesh):
    tiles = P("lat", "lon", None, None)
    return jax.shard_map(
        functools.partial(per_device, mesh.shape["lon"] // 2, mesh.shape["lat"]),
        mesh=mesh,
        in_specs=(tiles, tiles, tiles, tiles, P(), P()),
        out_specs=(tiles, tiles, tiles),
        check_vma=False,
    )
```

```python
import functools

import jax
import jax.numpy as jnp
from jax import lax
from jax.experimental import pallas as pl
from jax.experimental.pallas import tpu as pltpu
from jax.sharding import PartitionSpec as P

MESH = pl.DeviceIdType.MESH
PAIR_STEPS = (0, 1, -1, 2)
BANDS = (0, -1, 1)
BAND_BACK = (0, 2, 1)
UNLISTED = -1e30
LOWEST = -1e20
LOG2E = 1.4426950408889634


def dot_rows(a, b):
    return lax.dot_general(a, b, (((1,), (1,)), ((), ())), preferred_element_type=jnp.float32)


def dot(a, b):
    return jnp.dot(a, b, preferred_element_type=jnp.float32)


def kernel(
    pairs, bands,
    q_ref, k_ref, v_ref, g_ref, list_hbm, count_hbm,
    out_ref,
    qbuf, gbuf, kbuf, vbuf, kturn, pstore, gpstore, maxrow, bias, stats, stats_in,
    plow, dslow, dqacc, dkacc, dvacc, dqout, dqin, dkout, dvout, dkin, dvin,
    q_send, q_recv, g_send, g_recv, k_send, k_recv, v_send, v_recv, s_send, s_recv,
    dq_send, dq_recv, dk_send, dk_recv, dv_send, dv_recv,
    list_ref, count_ref, fetch_sem,
):
    rows, width = q_ref.shape[2], q_ref.shape[3]
    scale = width ** -0.5
    scale2 = scale * LOG2E
    lon = lax.axis_index("lon")
    lat = lax.axis_index("lat")
    g = lon // 2
    p = lon % 2
    sign = 1 - 2 * p
    ring = 2 * pairs

    def along(step):
        return lax.rem(lon + 2 * sign * step + 2 * ring, ring)

    def column(e):
        return 2 * g + p + e * sign

    own = ((q_ref.at[0, 0], qbuf.at[0]), (k_ref.at[0, 0], kbuf.at[0]),
           (v_ref.at[0, 0], vbuf.at[0]), (g_ref.at[0, 0], gbuf.at[0]),
           (list_hbm, list_ref), (count_hbm, count_ref))
    fetches = [
        pltpu.make_async_copy(src, dst, fetch_sem.at[i]) for i, (src, dst) in enumerate(own)
    ]
    for fetch in fetches:
        fetch.start()

    def has_band(place):
        below = jnp.where(place == 1, lat > 0, True)
        above = jnp.where(place == 2, lat < bands - 1, True)
        return jnp.logical_and(below, above)

    distances = sorted({e % pairs for e in range(-3, 4)} - {0})

    barrier = pltpu.get_barrier_semaphore()
    for e in distances:
        pl.semaphore_signal(barrier, inc=1, device_id={"lon": along(e), "lat": lat}, device_id_type=MESH)
    beside = [(0, 1), (0, 2), (1, 0)]
    for e, place in beside:
        @pl.when(has_band(place))
        def _(e=e, place=place):
            pl.semaphore_signal(
                barrier, inc=1,
                device_id={"lon": column(e), "lat": lat + BANDS[place]}, device_id_type=MESH,
            )

    n_beside = 1 + jnp.where(lat > 0, 1, 0) + jnp.where(lat < bands - 1, 1, 0)
    pl.semaphore_wait(barrier, len(distances) + n_beside)

    def remote(src, dst, send, recv, to_lon, to_lat):
        return pltpu.make_async_remote_copy(
            src_ref=src, dst_ref=dst, send_sem=send, recv_sem=recv,
            device_id={"lon": to_lon, "lat": to_lat}, device_id_type=MESH,
        )

    def key_copies(e, place):
        here, there = 3 * e + place, 3 * e + BAND_BACK[place]
        passed = e == 1 and place > 0
        to = (lon if passed else column(e), lat + BANDS[place])
        k_src = kbuf.at[3] if passed else k_ref.at[0, 0]
        v_src = vbuf.at[3] if passed else v_ref.at[0, 0]
        return (
            remote(k_src, kbuf.at[there], k_send.at[here], k_recv.at[there], *to),
            remote(v_src, vbuf.at[there], v_send.at[here], v_recv.at[there], *to),
        )

    line = pairs == 4
    inner = jnp.logical_and(g > 0, g < 3)
    inner_slot = jnp.where((g == 1) == (p == 0), 1, 2)

    def hand_on():
        to = (jnp.where(g == 1, lon - 2, lon + 2), lat)
        return (
            remote(qbuf.at[inner_slot], qbuf.at[3], q_send.at[3], q_recv.at[3], *to),
            remote(gbuf.at[inner_slot], gbuf.at[3], g_send.at[3], g_recv.at[3], *to),
        )

    def query_copies(t):
        to = (along(-PAIR_STEPS[t]), lat)
        return (
            remote(q_ref.at[0, 0], qbuf.at[t], q_send.at[t], q_recv.at[t], *to),
            remote(g_ref.at[0, 0], gbuf.at[t], g_send.at[t], g_recv.at[t], *to),
        )

    for t in (1, 2):
        for copy in query_copies(t):
            copy.start()

    @pl.when(jnp.logical_not(inner) if line else True)
    def _():
        for copy in query_copies(3):
            copy.start()

    for e, place in beside:
        @pl.when(has_band(place))
        def _(e=e, place=place):
            for copy in key_copies(e, place):
                copy.start()

    fetches[4].wait()
    fetches[5].wait()
    slot = lax.broadcasted_iota(jnp.int32, (8, 1), 0)
    other = jnp.where(slot >= 3, 1, 0)
    place = slot - 3 * other
    band = lat + jnp.where(place == 0, 0, jnp.where(place == 1, -1, 1))
    key_ids = band * ring + 2 * g + p + other * sign
    entry = lax.broadcasted_iota(jnp.int32, (1, list_ref.shape[2]), 1)
    lane = lax.broadcasted_iota(jnp.int32, (1, ring), 1)
    counts = count_ref[pl.ds(lat, 1), :]
    for t, step in enumerate(PAIR_STEPS):
        where_q = along(step)
        count = jnp.sum(jnp.where(lane == where_q, counts, 0), axis=1, keepdims=True)
        mine = list_ref[lat, pl.ds(where_q, 1), :]
        hit = jnp.where((mine == key_ids) & (entry < count), 1.0, 0.0)
        found = jnp.max(hit, axis=1, keepdims=True)
        bias[t] = jnp.broadcast_to(jnp.where(found > 0.5, 0.0, UNLISTED), (8, rows))

    stats[0:4] = jnp.full((4, rows), LOWEST, jnp.float32)
    stats[4:16] = jnp.zeros((12, rows), jnp.float32)

    dqacc[...] = jnp.zeros_like(dqacc)

    def arrived(buf, index, recv):
        pltpu.make_async_copy(buf.at[index], buf.at[index], recv.at[index]).wait()

    chunks = [pl.ds(i, 32) for i in range(0, rows, 32)]

    def first_slot(t):
        return 3 if t == 3 else 0

    def stored(t, ks):
        return t * 6 + ks - first_slot(t)

    def first_pair(t, ks):
        index = stored(t, ks)
        logits = dot_rows(kbuf[ks], qbuf[t])
        pstore[index] = logits
        offset = bias[t, pl.ds(ks, 1), :]
        top = jnp.max(logits, axis=0, keepdims=True) * scale2 + offset
        old = stats[t:t + 1]
        new = jnp.maximum(old, top)
        shift = new - offset
        gpstore[index] = dot_rows(vbuf[ks], gbuf[t])
        total = jnp.zeros((8, rows), jnp.float32)
        weighted = jnp.zeros((8, rows), jnp.float32)
        for c in chunks:
            powers = jnp.exp2(pstore[index, c, :] * scale2 - shift)
            pstore[index, c, :] = powers
            total += jnp.sum(powers.reshape(-1, 8, rows), axis=0)
            terms = powers * gpstore[index, c, :]
            weighted += jnp.sum(terms.reshape(-1, 8, rows), axis=0)
        total = jnp.sum(total, axis=0, keepdims=True)
        weighted = jnp.sum(weighted, axis=0, keepdims=True)
        shrink = jnp.exp2(old - new)
        maxrow[pl.ds(index, 1), :] = new
        stats[t:t + 1] = new
        stats[4 + t:5 + t] = stats[4 + t:5 + t] * shrink + total
        stats[8 + t:9 + t] = stats[8 + t:9 + t] * shrink + weighted

    for fetch in fetches[:4]:
        fetch.wait()

    def keys_arrive(ks):
        arrived(kbuf, ks, k_recv)
        arrived(vbuf, ks, v_recv)

    def turn(ks):
        kturn[ks] = kbuf[ks].astype(jnp.float32).T.astype(jnp.bfloat16)

    def first_pairs(ts, start, stop, fresh=False):
        def step(ks, carry):
            @pl.when(has_band(ks % 3))
            def _():
                if fresh:
                    keys_arrive(ks)
                    turn(ks)
                for t in ts:
                    first_pair(t, ks)
            return carry

        lax.fori_loop(start, stop, step, 0)

    turn(0)
    first_pair(0, 0)
    first_pairs((0,), 1, 3, fresh=True)
    keys_arrive(3)
    for place in (1, 2):
        @pl.when(has_band(place))
        def _(place=place):
            for copy in key_copies(1, place):
                copy.start()
    if line:
        @pl.when(inner)
        def _():
            arrived(qbuf, inner_slot, q_recv)
            arrived(gbuf, inner_slot, g_recv)
            for copy in hand_on():
                copy.start()

    turn(3)
    first_pair(0, 3)
    first_pairs((0,), 4, 6, fresh=True)
    for ts in ((1, 2), (3,)):
        for t in ts:
            taken = jnp.logical_and(inner, inner_slot == t)

            @pl.when(jnp.logical_not(taken) if line else True)
            def _(t=t):
                arrived(qbuf, t, q_recv)
                arrived(gbuf, t, g_recv)
        first_pairs(ts, first_slot(ts[0]), 6)

    def stat_copy(i, e):
        back = distances.index(-e % pairs)
        return remote(stats, stats_in.at[back], s_send.at[i], s_recv.at[back], along(e), lat)

    for i, e in enumerate(distances):
        stat_copy(i, e).start()
    for i, e in enumerate(distances):
        arrived(stats_in, i, s_recv)

    finals = []
    for t, step in enumerate(PAIR_STEPS):
        parts = [(stats[t:t + 1], stats[4 + t:5 + t], stats[8 + t:9 + t])]
        for i, e in enumerate(distances):
            for other_t, other_step in enumerate(PAIR_STEPS):
                if (other_step + e - step) % pairs == 0:
                    parts.append(tuple(
                        stats_in[i, r + other_t:r + other_t + 1, :] for r in (0, 4, 8)
                    ))
        top = functools.reduce(jnp.maximum, [m for m, _, _ in parts])
        total = sum(l * jnp.exp2(m - top) for m, l, _ in parts)
        weighted = sum(w * jnp.exp2(m - top) for m, _, w in parts)
        inverse = 1.0 / total
        finals.append((top, inverse, weighted * inverse))

    def low_terms(t, ks):
        index = stored(t, ks)
        top, inverse, delta = finals[t]
        factor = jnp.exp2(maxrow[pl.ds(index, 1), :] - top) * inverse
        columns = slice(t * rows, (t + 1) * rows)
        for c in chunks:
            probs = pstore[index, c, :] * factor
            plow[c, columns] = probs.astype(jnp.bfloat16)
            dslow[c, columns] = (probs * (gpstore[index, c, :] - delta)).astype(jnp.bfloat16)

    def products(first, count, ks):
        columns = slice(first * rows, (first + count) * rows)
        dqacc[:, columns] += dot(kturn[ks], dslow[:, columns])
        value_part = dot(plow[:, columns], gbuf[first:first + count].reshape(-1, width))
        key_part = dot(dslow[:, columns], qbuf[first:first + count].reshape(-1, width))
        return key_part, value_part

    def query_grad_copy(t):
        return remote(
            dqout.at[t], dqin.at[t], dq_send.at[t], dq_recv.at[t], along(PAIR_STEPS[t]), lat
        )

    def send_query_grad(t):
        dqout[t] = (dqacc[:, t * rows:(t + 1) * rows] * scale).astype(jnp.bfloat16)
        query_grad_copy(t).start()

    def key_grad_copies(ks):
        e, place = ks // 3, ks % 3
        back = 3 * e + jnp.where(place == 0, 0, 3 - place)
        to = (jnp.where(ks == 3, column(1), lon), lat + jnp.where(place == 0, 0, 2 * place - 3))
        return (
            remote(dkout.at[ks], dkin.at[back], dk_send.at[ks], dk_recv.at[back], *to),
            remote(dvout.at[ks], dvin.at[back], dv_send.at[ks], dv_recv.at[back], *to),
        )

    def send_key_grad(ks):
        dkout[ks] = (dkacc[ks] * scale).astype(jnp.bfloat16)
        dvout[ks] = dvacc[ks].astype(jnp.bfloat16)
        for copy in key_grad_copies(ks):
            copy.start()

    def add_key_grad(ks, into, factor):
        arrived(dkin, ks, dk_recv)
        arrived(dvin, ks, dv_recv)
        dkacc[into] += dkin[ks].astype(jnp.float32) * factor
        dvacc[into] += dvin[ks].astype(jnp.float32)

    def other_parity(i, carry):
        place = (i + 1) % 3
        ks = 3 + place

        @pl.when(has_band(place))
        def _():
            for t in (3, 2, 1, 0):
                low_terms(t, ks)
            key_late, value_late = products(2, 2, ks)
            key_early, value_early = products(0, 2, ks)
            dkacc[ks] = key_late + key_early
            dvacc[ks] = value_late + value_early

            @pl.when(place > 0)
            def _():
                send_key_grad(ks)
        return carry

    lax.fori_loop(0, 3, other_parity, 0)
    send_query_grad(3)

    def neighbours(ks):
        for t in (1, 2):
            low_terms(t, ks)
        dkacc[ks], dvacc[ks] = products(1, 2, ks)

    neighbours(0)
    for place in (1, 2):
        @pl.when(has_band(place))
        def _(place=place):
            add_key_grad(3 + place, 3, 1.0 / scale)
    send_key_grad(3)

    def same_parity(ks, carry):
        @pl.when(has_band(ks))
        def _():
            neighbours(ks)
        return carry

    lax.fori_loop(1, 3, same_parity, 0)
    send_query_grad(1)
    send_query_grad(2)

    def own_queries(i, carry):
        ks = (i + 1) % 3

        @pl.when(has_band(ks))
        def _():
            low_terms(0, ks)
            key_part, value_part = products(0, 1, ks)
            dkacc[ks] += key_part
            dvacc[ks] += value_part

            @pl.when(ks > 0)
            def _():
                send_key_grad(ks)
        return carry

    lax.fori_loop(0, 3, own_queries, 0)

    total = dqacc[:, :rows] * scale
    for t in (3, 1, 2):
        arrived(dqin, t, dq_recv)
        total += dqin[t].astype(jnp.float32)
    out_ref[0] = total.T.astype(jnp.bfloat16)

    add_key_grad(3, 0, 1.0 / scale)
    for place in (1, 2):
        @pl.when(has_band(place))
        def _(place=place):
            add_key_grad(place, 0, 1.0 / scale)
    out_ref[1] = (dkacc[0] * scale).astype(jnp.bfloat16)
    out_ref[2] = dvacc[0].astype(jnp.bfloat16)

    for t in (1, 2, 3):
        for copy in query_copies(t):
            copy.wait_send()
        query_grad_copy(t).wait_send()
    for i, e in enumerate(distances):
        stat_copy(i, e).wait_send()
    for e, place in beside + [(1, 1), (1, 2)]:
        @pl.when(has_band(place))
        def _(e=e, place=place):
            for copy in key_copies(e, place) + key_grad_copies(3 * e + place):
                copy.wait_send()


def per_device(pairs, bands, queries, keys, values, cotangent, key_tiles, tile_count):
    rows, width = queries.shape[2], queries.shape[3]
    low, full = jnp.bfloat16, jnp.float32
    n_stats = len({e % pairs for e in range(-3, 4)} - {0})
    vmem = pl.BlockSpec(memory_space=pltpu.VMEM)
    dma = pltpu.SemaphoreType.DMA
    grads = pl.pallas_call(
        functools.partial(kernel, pairs, bands),
        out_shape=jax.ShapeDtypeStruct((3, rows, width), low),
        in_specs=[pl.BlockSpec(memory_space=pl.ANY)] * 6,
        out_specs=vmem,
        scratch_shapes=[
            pltpu.VMEM((4, rows, width), low),
            pltpu.VMEM((4, rows, width), low),
            pltpu.VMEM((6, rows, width), low),
            pltpu.VMEM((6, rows, width), low),
            pltpu.VMEM((6, width, rows), low),
            pltpu.VMEM((21, rows, rows), full),
            pltpu.VMEM((21, rows, rows), full),
            pltpu.VMEM((24, rows), full),
            pltpu.VMEM((4, 8, rows), full),
            pltpu.VMEM((16, rows), full),
            pltpu.VMEM((n_stats, 16, rows), full),
            pltpu.VMEM((rows, 4 * rows), low),
            pltpu.VMEM((rows, 4 * rows), low),
            pltpu.VMEM((width, 4 * rows), full),
            pltpu.VMEM((6, rows, width), full),
            pltpu.VMEM((6, rows, width), full),
            pltpu.VMEM((4, width, rows), low),
            pltpu.VMEM((4, width, rows), low),
            pltpu.VMEM((6, rows, width), low),
            pltpu.VMEM((6, rows, width), low),
            pltpu.VMEM((6, rows, width), low),
            pltpu.VMEM((6, rows, width), low),
            dma((4,)), dma((4,)), dma((4,)), dma((4,)),
            dma((6,)), dma((6,)), dma((6,)), dma((6,)),
            dma((n_stats,)), dma((n_stats,)),
            dma((4,)), dma((4,)),
            dma((6,)), dma((6,)), dma((6,)), dma((6,)),
            pltpu.VMEM(key_tiles.shape, jnp.int32),
            pltpu.VMEM(tile_count.shape, jnp.int32),
            dma((6,)),
        ],
        compiler_params=pltpu.CompilerParams(
            collective_id=0, has_side_effects=True, vmem_limit_bytes=60 * 1024 * 1024
        ),
    )(queries, keys, values, cotangent, key_tiles, tile_count)
    return tuple(grads[i].reshape(queries.shape) for i in range(3))


def solution(mesh):
    tiles = P("lat", "lon", None, None)
    return jax.shard_map(
        functools.partial(per_device, mesh.shape["lon"] // 2, mesh.shape["lat"]),
        mesh=mesh,
        in_specs=(tiles, tiles, tiles, tiles, P(), P()),
        out_specs=(tiles, tiles, tiles),
        check_vma=False,
    )
```
